32 devices in a mesh: lat: 4 (over z), lon: 8 (over y, x, core).
Axes of the slice: x: 2, y: 2, z: 4, core: 2. Of those that a mesh axis runs over, the one named last changes fastest.
Arguments:
- radiances: bfloat16 [32768, 8461], P(('lat', 'lon')), may hold values from -6 to 6
- project_weight: bfloat16 [8461, 256], replicated, may hold values from -0.0625 to 0.0625
- tile_ids: int32 [32768], P(('lat', 'lon')), may hold values from 0 to 31, as said below
- slot_offsets: int32 [32768], P(('lat', 'lon')), may hold values from 0 to 2559, as said below
- tile_counts: int32 [4, 8], P('lat', 'lon'), may hold values from 512 to 2560, as said below
- setconv_weights: bfloat16 [256, 256, 2560], P('lat', 'lon'), may hold values from 0.049804688 to 1
- conv1_weight: bfloat16 [3, 3, 256, 256], replicated, may hold values from -0.125 to 0.125
- conv2_weight: bfloat16 [3, 3, 256, 256], replicated, may hold values from -0.125 to 0.125
Outputs:
- encoded: bfloat16 [64, 64, 256], P('lat', 'lon')
The draws below stay inside these ranges and needn't reach their ends.
Inputs may be any that keep to these rules, and one draw needn't show every extreme that they name: `tile_ids`: A device's observations bound for one tile stand next to each other; one device sends at most 112 observations to one tile, a number reached in every draw. `slot_offsets`: the observations bound for one tile hold the offsets 0 to its count minus 1, each once. `tile_counts`: each entry is the number of observations whose tile_ids name that tile; 2560 is reached in every draw.
All inputs are finite; a program needn't handle non-finite values.
Results may differ from the reference program's by a relative error of at most 0.009.
Values may be sent and summed in bfloat16 or wider, within the bound.
A program may use at most 512 MiB of HBM per device.

```python
import jax
import jax.numpy as jnp
import numpy as np
from jax import lax

CH_RAW = 8461
CHANNELS = 256
CLAT = 64
CLON = 32
OBS_DEV = 1024
SLOTS = 2560
OBSERVATIONS = 32768
NLAT = 256
NLON = 256
N_LAT = 4
N_LON = 8
DEVICES = 32


def observation_plan(key):
    unit_share = DEVICES // 16
    pair_mean = OBS_DEV // DEVICES
    level_table = np.concatenate([np.full(5 * unit_share, 0), np.full(3 * unit_share, 1), np.full(5 * unit_share, 3), np.full(2 * unit_share, 4), np.full(unit_share, 6)]).astype(np.int32)
    levels = jnp.asarray(level_table) * (pair_mean // 4)
    order = jax.random.permutation(jax.random.fold_in(key, 11), DEVICES)
    base_load = levels[order]
    hot_rank = jax.random.permutation(jax.random.fold_in(key, 12), DEVICES)
    hot_load = jnp.where(hot_rank < DEVICES // 4, 2 * pair_mean, 0).astype(jnp.int32)
    sources = jnp.arange(DEVICES, dtype=jnp.int32)[:, None]
    targets = jnp.arange(DEVICES, dtype=jnp.int32)[None, :]
    pair_load = base_load[(targets - sources) % DEVICES] + hot_load[None, :]
    tile_total = jnp.sum(pair_load, axis=0)
    pair_start = jnp.cumsum(pair_load, axis=0) - pair_load

    def one_loader(source):
        tile_order = (source + jnp.arange(DEVICES, dtype=jnp.int32)) % DEVICES
        run_length = pair_load[source, tile_order]
        run_begin = jnp.cumsum(run_length) - run_length
        run_index = jnp.repeat(jnp.arange(DEVICES, dtype=jnp.int32), run_length, total_repeat_length=OBS_DEV)
        loader_ids = tile_order[run_index]
        within_run = jnp.arange(OBS_DEV, dtype=jnp.int32) - run_begin[run_index]
        loader_offsets = pair_start[source, loader_ids] + within_run
        return (loader_ids, loader_offsets)
    all_ids, all_offsets = jax.vmap(one_loader)(jnp.arange(DEVICES, dtype=jnp.int32))
    return (all_ids.reshape(-1).astype(jnp.int32), all_offsets.reshape(-1).astype(jnp.int32), tile_total.astype(jnp.int32))


def draw_tile_ids(key, part):
    return observation_plan(key)[0]


def draw_slot_offsets(key, part):
    return observation_plan(key)[1]


def draw_tile_counts(key, part):
    return observation_plan(key)[2].reshape(-1, NLON // CLON)


def shard_levels(stream_key, extent, cuts, smallest, top_value):
    def one(axis_at, shards_of):
        steps = jax.random.uniform(jax.random.fold_in(jax.random.fold_in(stream_key, 6), axis_at), (shards_of,), jnp.float32, smallest / len(cuts), top_value / len(cuts))
        return jnp.repeat(jnp.exp(steps), extent[axis_at] // shards_of).reshape((-1,) + (1,) * (len(extent) - axis_at - 1))

    loudness = one(*cuts[0])
    for cut in cuts[1:]:
        loudness = loudness * one(*cut)
    return loudness


def normal_values(rng, shape, width, reach, split=(), held_as=jnp.bfloat16):
    drawn = width * jax.random.normal(rng, shape, jnp.float32)
    if split:
        drawn = drawn * shard_levels(rng, shape, split, -0.22, 0.18)
    return jnp.clip(drawn, -reach, reach).astype(held_as)


def setup_inputs(seed: int = 0) -> dict:
    key_list = jax.random.split(jax.random.key(seed), 9)
    return {
        "radiances": normal_values(key_list[0], (OBSERVATIONS, CH_RAW), 1.0, 6.0, ((0, 32),)),
        "project_weight": normal_values(key_list[1], (CH_RAW, CHANNELS), CH_RAW ** -0.5, 0.0625),
        "tile_ids": draw_tile_ids(jax.random.fold_in(key_list[8], 71), 0),
        "slot_offsets": draw_slot_offsets(jax.random.fold_in(key_list[8], 71), 0),
        "tile_counts": draw_tile_counts(jax.random.fold_in(key_list[8], 71), 0),
        "setconv_weights": jnp.clip(0.049804688 + 0.9501953 * jax.random.uniform(key_list[5], (NLAT, NLON, SLOTS), jnp.float32) ** shard_levels(key_list[5], (NLAT, NLON, SLOTS), ((0, 4), (1, 8)), -0.2, 0.2), 0.049804688, 1.0).astype(jnp.bfloat16),
        "conv1_weight": normal_values(key_list[6], (3, 3, CHANNELS, CHANNELS), (9 * CHANNELS) ** -0.5, 0.125),
        "conv2_weight": normal_values(key_list[7], (3, 3, CHANNELS, CHANNELS), (9 * CHANNELS) ** -0.5, 0.125),
    }


def project_rows(radiances, project_weight):
    blocks = radiances.reshape(-1, OBS_DEV, radiances.shape[1])

    def one_block(rows):
        return jnp.dot(rows, project_weight, preferred_element_type=jnp.float32).astype(jnp.bfloat16)
    return lax.map(one_block, blocks).reshape(-1, project_weight.shape[1])

def stride_conv(field, kernel):
    height, breadth, depth = field.shape
    upper_rim = jnp.zeros((1, breadth, depth), field.dtype)
    extended = jnp.concatenate([upper_rim, field], axis=0)
    padded = jnp.concatenate([extended[:, -1:], extended], axis=1)
    out_rows, out_cols = (height // 2, breadth // 2)
    summed = jnp.zeros((out_rows * out_cols, depth), jnp.float32)
    for row_tap in range(3):
        for col_tap in range(3):
            window = padded[row_tap:row_tap + 2 * out_rows:2, col_tap:col_tap + 2 * out_cols:2].reshape(-1, depth)
            summed = summed + jnp.dot(window, kernel[row_tap, col_tap], preferred_element_type=jnp.float32)
    return summed.reshape(out_rows, out_cols, depth)

def reference(radiances, project_weight, tile_ids, slot_offsets, tile_counts, setconv_weights, conv1_weight, conv2_weight):
    channel_count = project_weight.shape[1]
    features = project_rows(radiances, project_weight)
    tile_total = N_LAT * N_LON
    flat_block = jnp.zeros((tile_total * SLOTS, channel_count), jnp.bfloat16)
    flat_block = flat_block.at[(tile_ids * SLOTS + slot_offsets).astype(jnp.int32)].set(features)
    obs_block = flat_block.reshape(tile_total, SLOTS, channel_count)
    tile_weights = setconv_weights.reshape(N_LAT, CLAT, N_LON, CLON, SLOTS).transpose(0, 2, 1, 3, 4)
    tile_weights = tile_weights.reshape(tile_total, CLAT * CLON, SLOTS)
    counts_flat = tile_counts.reshape(-1).astype(jnp.int32)

    def one_tile(operands):
        weights_tile, block_tile, tile_count = operands
        live_mask = jnp.arange(SLOTS, dtype=jnp.int32) < tile_count
        masked = jnp.where(live_mask[None, :], weights_tile, jnp.zeros((), weights_tile.dtype))
        numerator = jnp.dot(masked, block_tile, preferred_element_type=jnp.float32)
        density = lax.optimization_barrier(jnp.sum(masked, axis=1, dtype=jnp.float32))
        return (numerator / jnp.sqrt(density)[:, None]).astype(jnp.bfloat16)
    tiles_out = lax.map(one_tile, (tile_weights, obs_block, counts_flat))
    grid = tiles_out.reshape(N_LAT, N_LON, CLAT, CLON, channel_count).transpose(0, 2, 1, 3, 4)
    grid = grid.reshape(NLAT, NLON, channel_count)
    hidden = jax.nn.gelu(stride_conv(grid, conv1_weight)).astype(jnp.bfloat16)
    return stride_conv(hidden, conv2_weight).astype(jnp.bfloat16)
```

```python
import functools

import jax
import jax.numpy as jnp
from jax import lax
from jax.experimental import pallas as pl
from jax.experimental.pallas import tpu as pltpu
from jax.sharding import PartitionSpec as P

MESH = pl.DeviceIdType.MESH
MIB = 1024 * 1024


def project_pack_kernel(steps, rows, rad_ref, weight_ref, pos_ref, packed_ref, feat_ref):
    step = pl.program_id(0)
    feat_ref[pl.ds(pl.multiple_of(step * rows, rows), rows), :] = jnp.dot(
        rad_ref[...], weight_ref[...], preferred_element_type=jnp.float32
    ).astype(jnp.bfloat16)

    @pl.when(step == steps - 1)
    def _():
        total = packed_ref.shape[0]
        chunk = 256 if total % 256 == 0 else 128
        obs = feat_ref.shape[0]

        @pl.loop(0, total // chunk)
        def _(c):
            base = pl.multiple_of(c * chunk, chunk)
            target = lax.broadcasted_iota(jnp.int32, (chunk, obs), 0) + base
            onehot = (target == pos_ref[...]).astype(jnp.float32).astype(jnp.bfloat16)
            packed_ref[pl.ds(base, chunk), :] = jnp.dot(
                onehot, feat_ref[...], preferred_element_type=jnp.float32
            ).astype(jnp.bfloat16)


def project_pack(radiances, weight, pos, total):
    obs, raw = radiances.shape
    channels = weight.shape[1]
    rows = 256
    steps = obs // rows
    return pl.pallas_call(
        functools.partial(project_pack_kernel, steps, rows),
        grid=(steps,),
        out_shape=jax.ShapeDtypeStruct((total, channels), jnp.bfloat16),
        in_specs=[
            pl.BlockSpec((rows, raw), lambda i: (i, 0)),
            pl.BlockSpec((raw, channels), lambda i: (0, 0)),
            pl.BlockSpec((1, obs), lambda i: (0, 0)),
        ],
        out_specs=pl.BlockSpec((total, channels), lambda i: (0, 0)),
        scratch_shapes=[pltpu.VMEM((obs, channels), jnp.bfloat16)],
        compiler_params=pltpu.CompilerParams(vmem_limit_bytes=48 * MIB),
        cost_estimate=pl.CostEstimate(
            flops=2 * obs * raw * channels,
            bytes_accessed=2 * (obs * raw + raw * channels + total * channels),
            transcendentals=0,
        ),
        name="project_pack",
    )(radiances, weight, pos)


def setconv_kernel(
    n_lat, n_lon, cap, group, chunk,
    packed_ref, slots_ref, live_ref, w_hbm, out_ref,
    arrived, w_vmem, obs, dens, send_sem, recv_sem, own_sem, w_sem,
):
    n = n_lat * n_lon
    me = lax.axis_index("lat") * n_lon + lax.axis_index("lon")
    cells, slot_count = w_vmem.shape
    chunks = cells // chunk

    def w_copy(c):
        part = pl.ds(pl.multiple_of(c * chunk, chunk), chunk)
        return pltpu.make_async_copy(w_hbm.at[part], w_vmem.at[part], w_sem.at[c])

    def send(d):
        peer = lax.rem(me + d, n)
        return pltpu.make_async_remote_copy(
            src_ref=packed_ref.at[peer],
            dst_ref=arrived.at[me],
            send_sem=send_sem.at[d],
            recv_sem=recv_sem.at[me],
            device_id=(peer // n_lon, lax.rem(peer, n_lon)),
            device_id_type=MESH,
        )

    def arrival(source):
        return pltpu.make_async_remote_copy(
            src_ref=packed_ref.at[source],
            dst_ref=arrived.at[source],
            send_sem=send_sem.at[0],
            recv_sem=recv_sem.at[source],
            device_id=(source // n_lon, lax.rem(source, n_lon)),
            device_id_type=MESH,
        )

    barrier = pltpu.get_barrier_semaphore()

    @pl.loop(1, n)
    def _(d):
        peer = lax.rem(me + d, n)
        pl.semaphore_signal(
            barrier, inc=1, device_id=(peer // n_lon, lax.rem(peer, n_lon)), device_id_type=MESH
        )

    own = pltpu.make_async_copy(packed_ref.at[me], arrived.at[me], own_sem)
    own.start()
    pl.semaphore_wait(barrier, n - 1)

    @pl.loop(1, n)
    def _(d):
        send(d).start()

    @pl.loop(0, chunks)
    def _(c):
        w_copy(c).start()

    obs[...] = jnp.zeros_like(obs)

    @pl.loop(0, chunks)
    def _(c):
        w_copy(c).wait()
        part = pl.ds(pl.multiple_of(c * chunk, chunk), chunk)
        dens[part, :] = jnp.dot(
            w_vmem[part, :], live_ref[...], preferred_element_type=jnp.float32
        )

    own.wait()
    width = group * cap
    groups = n // group
    obs_chunk = 256

    @pl.loop(0, groups)
    def _(k):
        g = lax.rem(me // group + k, groups)
        for j in range(group):
            source = g * group + j

            @pl.when(source != me)
            def _():
                arrival(source).wait_recv()

        rows = arrived[pl.ds(g * group, group)].reshape(width, arrived.shape[2])
        slots = slots_ref[g]

        @pl.loop(0, slot_count // obs_chunk)
        def _(c):
            base = pl.multiple_of(c * obs_chunk, obs_chunk)
            at = lax.broadcasted_iota(jnp.int32, (obs_chunk, width), 0) + base
            onehot = (at == slots).astype(jnp.float32).astype(jnp.bfloat16)
            placed = jnp.dot(onehot, rows, preferred_element_type=jnp.float32)
            obs[pl.ds(base, obs_chunk), :] += placed.astype(jnp.bfloat16)

    @pl.loop(0, chunks)
    def _(c):
        part = pl.ds(pl.multiple_of(c * chunk, chunk), chunk)
        numerator = jnp.dot(w_vmem[part, :], obs[...], preferred_element_type=jnp.float32)
        root = jnp.sqrt(dens[part, :])
        root = jnp.concatenate([root] * (numerator.shape[1] // root.shape[1]), axis=1)
        out_ref[part, :] = (numerator / root).astype(jnp.bfloat16)

    @pl.loop(1, n)
    def _(d):
        send(d).wait_send()


def setconv(packed, slots, live, weights, n_lat, n_lon, cap, group):
    n = n_lat * n_lon
    channels = packed.shape[2]
    cells, slot_count = weights.shape
    chunk = 256
    vmem = pl.BlockSpec(memory_space=pltpu.VMEM)
    return pl.pallas_call(
        functools.partial(setconv_kernel, n_lat, n_lon, cap, group, chunk),
        out_shape=jax.ShapeDtypeStruct((cells, channels), jnp.bfloat16),
        in_specs=[vmem, vmem, vmem, pl.BlockSpec(memory_space=pl.ANY)],
        out_specs=vmem,
        scratch_shapes=[
            pltpu.VMEM((n, cap, channels), jnp.bfloat16),
            pltpu.VMEM((cells, slot_count), jnp.bfloat16),
            pltpu.VMEM((slot_count, channels), jnp.bfloat16),
            pltpu.VMEM((cells, 128), jnp.float32),
            pltpu.SemaphoreType.DMA((n,)),
            pltpu.SemaphoreType.DMA((n,)),
            pltpu.SemaphoreType.DMA,
            pltpu.SemaphoreType.DMA((cells // chunk,)),
        ],
        compiler_params=pltpu.CompilerParams(
            collective_id=0, has_side_effects=True, vmem_limit_bytes=48 * MIB
        ),
        cost_estimate=pl.CostEstimate(
            flops=4 * cells * slot_count * channels,
            bytes_accessed=2 * cells * slot_count,
            transcendentals=0,
        ),
        name="setconv",
    )(packed, slots, live, weights)


def load_rows(ref, rows):
    return jnp.concatenate([ref[h, rows, :] for h in range(ref.shape[0])], axis=1)


def store_rows(ref, rows, value):
    for h in range(ref.shape[0]):
        ref[h, rows, :] = value[:, h * 128:(h + 1) * 128]


def conv_stage(first, n_lat, n_lon, lat, lon, field, weight, height, width,
               even, odd, column, west, corner, shift, sems):
    half = width // 2
    depth = even.shape[2]
    pairs = height * half
    even[1:, :, :] = load_rows(field, pl.ds(0, pairs, stride=2)).reshape(height, half, depth)
    odd[1:, :, :] = load_rows(field, pl.ds(1, pairs, stride=2)).reshape(height, half, depth)
    store_rows(column, pl.ds(0, height), load_rows(field, pl.ds(width - 1, height, stride=width)))
    below = lax.rem(lat + 1, n_lat)
    east = lax.rem(lon + 1, n_lon)

    def copy(src, dst, k, device):
        return pltpu.make_async_remote_copy(
            src_ref=src, dst_ref=dst, send_sem=sems.at[0, first + k],
            recv_sem=sems.at[1, first + k], device_id=device, device_id_type=MESH,
        )

    sideways = copy(column, west.at[:, pl.ds(8, height)], 0, (lat, east))
    downward = [
        copy(odd.at[height], odd.at[0], 1, (below, lon)),
        copy(even.at[height], even.at[0], 2, (below, lon)),
        copy(odd.at[height], corner, 3, (below, east)),
    ]

    @pl.when(lat < n_lat - 1)
    def _():
        for item in downward:
            item.start()

    sideways.start()

    @pl.when(lat == 0)
    def _():
        even[0] = jnp.zeros_like(even[0])
        odd[0] = jnp.zeros_like(odd[0])
        corner[...] = jnp.zeros_like(corner)

    out_rows = height // 2
    flat = out_rows * half

    def rows_of(ref, tap):
        start = 1 if tap else 0
        picked = ref[start:start + 2 * out_rows].reshape(out_rows, 2, half, depth)
        return picked[:, tap - start].reshape(flat, depth).astype(jnp.bfloat16)

    def dot(rows, a, b):
        return jnp.dot(rows, weight[a, b], preferred_element_type=jnp.float32)

    central = None
    westward = None
    for tap in (1, 2, 0):
        if tap == 0:
            @pl.when(lat > 0)
            def _():
                for item in downward:
                    item.wait_recv()
        odd_rows = rows_of(odd, tap)
        c = dot(rows_of(even, tap), tap, 1) + dot(odd_rows, tap, 2)
        w = dot(odd_rows, tap, 0)
        central = c if central is None else central + c
        westward = w if westward is None else westward + w
    store_rows(shift, pl.ds(8, flat), westward)
    sideways.wait_recv()
    store_rows(west, pl.ds(7, 1), corner[half - 1:half, :])
    rim = jnp.zeros((out_rows, depth), jnp.float32)
    for tap in range(3):
        taken = load_rows(west, pl.ds(7 + tap, out_rows, stride=2)).astype(jnp.bfloat16)
        rim = rim + dot(taken, tap, 0)
    store_rows(shift, pl.ds(7, out_rows, stride=half), rim)
    result = central + load_rows(shift, pl.ds(7, flat))

    @pl.when(lat < n_lat - 1)
    def _():
        for item in downward:
            item.wait_send()

    sideways.wait_send()
    return result


def encode_kernel(
    n_lat, n_lon, height, width, grid_ref, k1_ref, k2_ref, out_ref,
    field1, even1, odd1, col1, west1, corner1, shift1,
    field2, even2, odd2, col2, west2, corner2, shift2, sems,
):
    lat = lax.axis_index("lat")
    lon = lax.axis_index("lon")
    barrier = pltpu.get_barrier_semaphore()
    below = lax.rem(lat + 1, n_lat)
    above = lax.rem(lat + n_lat - 1, n_lat)
    east = lax.rem(lon + 1, n_lon)
    west = lax.rem(lon + n_lon - 1, n_lon)
    peers = [(lat, east), (lat, west), (below, lon), (above, lon), (below, east), (above, west)]
    for peer in peers:
        pl.semaphore_signal(barrier, inc=1, device_id=peer, device_id_type=MESH)
    store_rows(field1, pl.ds(0, height * width), grid_ref[...].astype(jnp.float32))
    pl.semaphore_wait(barrier, len(peers))
    first = conv_stage(0, n_lat, n_lon, lat, lon, field1, k1_ref, height, width,
                       even1, odd1, col1, west1, corner1, shift1, sems)
    hidden = jax.nn.gelu(first).astype(jnp.bfloat16)
    store_rows(field2, pl.ds(0, height * width // 4), hidden.astype(jnp.float32))
    second = conv_stage(4, n_lat, n_lon, lat, lon, field2, k2_ref, height // 2, width // 2,
                        even2, odd2, col2, west2, corner2, shift2, sems)
    out_ref[...] = second.astype(jnp.bfloat16)


def encode(grid, kernel1, kernel2, n_lat, n_lon, height, width):
    depth = grid.shape[1]
    vmem = pl.BlockSpec(memory_space=pltpu.VMEM)

    def scratch(h, w):
        f32 = lambda *shape: pltpu.VMEM(shape, jnp.float32)
        lanes = depth // 128
        return [
            f32(lanes, h * w, 128), f32(h + 1, w // 2, depth), f32(h + 1, w // 2, depth),
            f32(lanes, h, 128), f32(lanes, h + 8, 128), f32(w // 2, depth),
            f32(lanes, h * w // 4 + 8, 128),
        ]

    return pl.pallas_call(
        functools.partial(encode_kernel, n_lat, n_lon, height, width),
        out_shape=jax.ShapeDtypeStruct((height * width // 16, depth), jnp.bfloat16),
        in_specs=[vmem] * 3,
        out_specs=vmem,
        scratch_shapes=scratch(height, width) + scratch(height // 2, width // 2)
        + [pltpu.SemaphoreType.DMA((2, 8))],
        compiler_params=pltpu.CompilerParams(
            collective_id=1, has_side_effects=True, vmem_limit_bytes=48 * MIB
        ),
        name="encode",
    )(grid, kernel1, kernel2)


def body(
    radiances, project_weight, tile_ids, slot_offsets, tile_counts,
    setconv_weights, conv1_weight, conv2_weight,
):
    n_lat = lax.axis_size("lat")
    n_lon = lax.axis_size("lon")
    n = n_lat * n_lon
    obs_count = radiances.shape[0]
    limit = 7 * (obs_count // n) // 2
    cap = -(-limit // 16) * 16
    group = max(1, 256 // cap)
    tile_rows, tile_cols, slot_count = setconv_weights.shape
    channels = project_weight.shape[1]

    place = jnp.arange(obs_count, dtype=jnp.int32) % cap
    pos = (tile_ids * cap + place).reshape(1, obs_count)
    keys = lax.all_gather(tile_ids * 4096 + slot_offsets, ("lat", "lon"))
    packed = project_pack(radiances, project_weight, pos, n * cap)

    me = lax.axis_index("lat") * n_lon + lax.axis_index("lon")
    turns = -(-obs_count // cap)
    keys = jnp.pad(keys, ((0, 0), (0, turns * cap - obs_count)), constant_values=-1)
    keys = keys.reshape(n, turns, cap)
    slots = jnp.max(jnp.where(keys // 4096 == me, keys % 4096, -1), axis=1)
    slots = slots.reshape(n // group, 1, group * cap)
    live = jnp.arange(slot_count, dtype=jnp.int32) < tile_counts.reshape(-1)[0]
    live = jnp.broadcast_to(live[:, None], (slot_count, 128)).astype(jnp.bfloat16)
    grid = setconv(
        packed.reshape(n, cap, channels), slots, live,
        setconv_weights.reshape(-1, slot_count), n_lat, n_lon, cap, group,
    )
    out = encode(grid, conv1_weight, conv2_weight, n_lat, n_lon, tile_rows, tile_cols)
    return out.reshape(tile_rows // 4, tile_cols // 4, channels)


def solution(mesh):
    in_specs = (
        P(("lat", "lon"), None),
        P(),
        P(("lat", "lon")),
        P(("lat", "lon")),
        P("lat", "lon"),
        P("lat", "lon", None),
        P(),
        P(),
    )
    out_specs = P("lat", "lon", None)
    return jax.shard_map(body, mesh=mesh, in_specs=in_specs, out_specs=out_specs, check_vma=False)
```

```python
import functools

import jax
import jax.numpy as jnp
from jax import lax
from jax.experimental import pallas as pl
from jax.experimental.pallas import tpu as pltpu
from jax.sharding import PartitionSpec as P

MESH = pl.DeviceIdType.MESH
MIB = 1024 * 1024


def project_pack_kernel(steps, tail, rad_ref, weight_ref, pos_ref, packed_ref, acc_ref, feat_ref):
    step = pl.program_id(0)

    def part(weight, rows):
        return lax.dot_general(
            weight, rows, (((0,), (0,)), ((), ())), preferred_element_type=jnp.float32
        )

    @pl.when(step == 0)
    def _():
        acc_ref[...] = part(weight_ref[...], rad_ref[...])

    @pl.when((step > 0) & (step < steps - 1))
    def _():
        acc_ref[...] += part(weight_ref[...], rad_ref[...])

    @pl.when(step == steps - 1)
    def _():
        last = acc_ref[...] + part(weight_ref[:tail], rad_ref[:tail])
        feat_ref[...] = last.T.astype(jnp.bfloat16)
        total = packed_ref.shape[0]
        chunk = 256 if total % 256 == 0 else 128
        obs = feat_ref.shape[0]

        @pl.loop(0, total // chunk)
        def _(c):
            base = pl.multiple_of(c * chunk, chunk)
            target = lax.broadcasted_iota(jnp.int32, (chunk, obs), 0) + base
            onehot = (target == pos_ref[...]).astype(jnp.float32).astype(jnp.bfloat16)
            packed_ref[pl.ds(base, chunk), :] = jnp.dot(
                onehot, feat_ref[...], preferred_element_type=jnp.float32
            ).astype(jnp.bfloat16)


def project_pack(radiances, weight, pos, total):
    raw, obs = radiances.shape
    channels = weight.shape[1]
    block = 1024
    steps = -(-raw // block)
    return pl.pallas_call(
        functools.partial(project_pack_kernel, steps, raw - (steps - 1) * block),
        grid=(steps,),
        out_shape=jax.ShapeDtypeStruct((total, channels), jnp.bfloat16),
        in_specs=[
            pl.BlockSpec((block, obs), lambda i: (i, 0)),
            pl.BlockSpec((block, channels), lambda i: (i, 0)),
            pl.BlockSpec((1, obs), lambda i: (0, 0)),
        ],
        out_specs=pl.BlockSpec((total, channels), lambda i: (0, 0)),
        scratch_shapes=[
            pltpu.VMEM((channels, obs), jnp.float32),
            pltpu.VMEM((obs, channels), jnp.bfloat16),
        ],
        compiler_params=pltpu.CompilerParams(vmem_limit_bytes=48 * MIB),
        cost_estimate=pl.CostEstimate(
            flops=2 * obs * raw * channels,
            bytes_accessed=2 * (obs * raw + raw * channels + total * channels),
            transcendentals=0,
        ),
        name="project_pack",
    )(radiances, weight, pos)


def flipped(value, by, count):
    result = 0
    bit = 1
    while bit < count:
        result = result + lax.rem(value // bit + by // bit, 2) * bit
        bit *= 2
    return result


def setconv_kernel(
    n_lat, n_lon, cap, chunk,
    packed_ref, slots_ref, live_ref, w_hbm, out_ref,
    arrived, slots_in, w_vmem, obs, dens,
    send_sem, recv_sem, slot_send_sem, slot_recv_sem, own_sem, w_sem,
):
    n = n_lat * n_lon
    lat = lax.axis_index("lat")
    lon = lax.axis_index("lon")
    me = lat * n_lon + lon
    cells, slot_count = w_vmem.shape
    chunks = cells // chunk

    def w_copy(c):
        part = pl.ds(pl.multiple_of(c * chunk, chunk), chunk)
        return pltpu.make_async_copy(w_hbm.at[part], w_vmem.at[part], w_sem.at[c])

    def partner(j):
        d = lax.rem(11 * j, n)
        return flipped(lat, d // n_lon, n_lat), flipped(lon, lax.rem(d, n_lon), n_lon)

    def number(j):
        peer_lat, peer_lon = partner(j)
        return peer_lat * n_lon + peer_lon

    def row_copy(j, slot):
        return pltpu.make_async_remote_copy(
            src_ref=packed_ref.at[number(j)],
            dst_ref=arrived.at[slot, pl.ds(0, cap)],
            send_sem=send_sem.at[j],
            recv_sem=recv_sem.at[slot],
            device_id=partner(j),
            device_id_type=MESH,
        )

    def slot_copy(j, slot):
        return pltpu.make_async_remote_copy(
            src_ref=slots_ref.at[number(j)],
            dst_ref=slots_in.at[slot],
            send_sem=slot_send_sem.at[j],
            recv_sem=slot_recv_sem.at[slot],
            device_id=partner(j),
            device_id_type=MESH,
        )

    barrier = pltpu.get_barrier_semaphore()

    @pl.loop(1, n)
    def _(j):
        pl.semaphore_signal(barrier, inc=1, device_id=partner(j), device_id_type=MESH)

    own_rows = pltpu.make_async_copy(
        packed_ref.at[me], arrived.at[me, pl.ds(0, cap)], own_sem.at[0]
    )
    own_slots = pltpu.make_async_copy(slots_ref.at[me], slots_in.at[me], own_sem.at[1])
    own_rows.start()
    own_slots.start()
    padding = arrived.shape[1] - cap
    if padding:
        arrived[:, cap:, :] = jnp.zeros((n, padding, arrived.shape[2]), jnp.bfloat16)
    pl.semaphore_wait(barrier, n - 1)

    @pl.loop(1, n)
    def _(j):
        row_copy(j, me).start()

    @pl.loop(1, n)
    def _(j):
        slot_copy(j, me).start()

    @pl.loop(0, chunks)
    def _(c):
        w_copy(c).start()

    obs[...] = jnp.zeros_like(obs)

    @pl.loop(0, chunks)
    def _(c):
        w_copy(c).wait()
        part = pl.ds(pl.multiple_of(c * chunk, chunk), chunk)
        dens[part, :] = jnp.dot(
            w_vmem[part, :], live_ref[...], preferred_element_type=jnp.float32
        )

    own_rows.wait()
    own_slots.wait()
    obs_chunk = 256

    @pl.loop(0, n // 2)
    def _(k):
        sources = [number(2 * k), number(2 * k + 1)]

        @pl.when(k > 0)
        def _():
            slot_copy(2 * k, sources[0]).wait_recv()
            row_copy(2 * k, sources[0]).wait_recv()

        slot_copy(2 * k + 1, sources[1]).wait_recv()
        row_copy(2 * k + 1, sources[1]).wait_recv()
        rows = jnp.concatenate([arrived[source] for source in sources], axis=0)
        slots = jnp.concatenate([slots_in[source] for source in sources], axis=1)

        @pl.loop(0, slot_count // obs_chunk)
        def _(c):
            base = pl.multiple_of(c * obs_chunk, obs_chunk)
            at = lax.broadcasted_iota(jnp.int32, (obs_chunk, slots.shape[1]), 0) + base
            onehot = (at == slots).astype(jnp.float32).astype(jnp.bfloat16)
            placed = jnp.dot(onehot, rows, preferred_element_type=jnp.float32)
            obs[pl.ds(base, obs_chunk), :] += placed.astype(jnp.bfloat16)

    @pl.loop(0, chunks)
    def _(c):
        part = pl.ds(pl.multiple_of(c * chunk, chunk), chunk)
        numerator = jnp.dot(w_vmem[part, :], obs[...], preferred_element_type=jnp.float32)
        root = jnp.sqrt(dens[part, :])
        root = jnp.concatenate([root] * (numerator.shape[1] // root.shape[1]), axis=1)
        out_ref[part, :] = (numerator / root).astype(jnp.bfloat16)

    @pl.loop(1, n)
    def _(j):
        row_copy(j, me).wait_send()
        slot_copy(j, me).wait_send()


def setconv(packed, slots, live, weights, n_lat, n_lon):
    n, cap, channels = packed.shape
    lanes = slots.shape[2]
    cells, slot_count = weights.shape
    chunk = 256
    vmem = pl.BlockSpec(memory_space=pltpu.VMEM)
    return pl.pallas_call(
        functools.partial(setconv_kernel, n_lat, n_lon, cap, chunk),
        out_shape=jax.ShapeDtypeStruct((cells, channels), jnp.bfloat16),
        in_specs=[vmem, vmem, vmem, pl.BlockSpec(memory_space=pl.ANY)],
        out_specs=vmem,
        scratch_shapes=[
            pltpu.VMEM((n, lanes, channels), jnp.bfloat16),
            pltpu.VMEM((n, 1, lanes), jnp.int32),
            pltpu.VMEM((cells, slot_count), jnp.bfloat16),
            pltpu.VMEM((slot_count, channels), jnp.bfloat16),
            pltpu.VMEM((cells, 128), jnp.float32),
            pltpu.SemaphoreType.DMA((n,)),
            pltpu.SemaphoreType.DMA((n,)),
            pltpu.SemaphoreType.DMA((n,)),
            pltpu.SemaphoreType.DMA((n,)),
            pltpu.SemaphoreType.DMA((2,)),
            pltpu.SemaphoreType.DMA((cells // chunk,)),
        ],
        compiler_params=pltpu.CompilerParams(
            collective_id=0, has_side_effects=True, vmem_limit_bytes=48 * MIB
        ),
        cost_estimate=pl.CostEstimate(
            flops=4 * cells * slot_count * channels,
            bytes_accessed=2 * cells * slot_count,
            transcendentals=0,
        ),
        name="setconv",
    )(packed, slots, live, weights)


def load_rows(ref, rows):
    return jnp.concatenate([ref[h, rows, :] for h in range(ref.shape[0])], axis=1)


def store_rows(ref, rows, value):
    for h in range(ref.shape[0]):
        ref[h, rows, :] = value[:, h * 128:(h + 1) * 128]


def conv_stage(first, n_lat, n_lon, lat, lon, field, weight, height, width,
               even, odd, column, west, corner, shift, sems):
    half = width // 2
    depth = even.shape[2]
    pairs = height * half
    even[1:, :, :] = load_rows(field, pl.ds(0, pairs, stride=2)).reshape(height, half, depth)
    odd[1:, :, :] = load_rows(field, pl.ds(1, pairs, stride=2)).reshape(height, half, depth)
    store_rows(column, pl.ds(0, height), load_rows(field, pl.ds(width - 1, height, stride=width)))
    below = lax.rem(lat + 1, n_lat)
    east = lax.rem(lon + 1, n_lon)

    def copy(src, dst, k, device):
        return pltpu.make_async_remote_copy(
            src_ref=src, dst_ref=dst, send_sem=sems.at[0, first + k],
            recv_sem=sems.at[1, first + k], device_id=device, device_id_type=MESH,
        )

    sideways = copy(column, west.at[:, pl.ds(8, height)], 0, (lat, east))
    downward = [
        copy(odd.at[height], odd.at[0], 1, (below, lon)),
        copy(even.at[height], even.at[0], 2, (below, lon)),
        copy(odd.at[height], corner, 3, (below, east)),
    ]

    @pl.when(lat < n_lat - 1)
    def _():
        for item in downward:
            item.start()

    sideways.start()

    @pl.when(lat == 0)
    def _():
        even[0] = jnp.zeros_like(even[0])
        odd[0] = jnp.zeros_like(odd[0])
        corner[...] = jnp.zeros_like(corner)

    out_rows = height // 2
    flat = out_rows * half

    def rows_of(ref, tap):
        start = 1 if tap else 0
        picked = ref[start:start + 2 * out_rows].reshape(out_rows, 2, half, depth)
        return picked[:, tap - start].reshape(flat, depth).astype(jnp.bfloat16)

    def dot(rows, a, b):
        return jnp.dot(rows, weight[a, b], preferred_element_type=jnp.float32)

    central = None
    westward = None
    for tap in (1, 2, 0):
        if tap == 0:
            @pl.when(lat > 0)
            def _():
                for item in downward:
                    item.wait_recv()
        odd_rows = rows_of(odd, tap)
        c = dot(rows_of(even, tap), tap, 1) + dot(odd_rows, tap, 2)
        w = dot(odd_rows, tap, 0)
        central = c if central is None else central + c
        westward = w if westward is None else westward + w
    store_rows(shift, pl.ds(8, flat), westward)
    sideways.wait_recv()
    store_rows(west, pl.ds(7, 1), corner[half - 1:half, :])
    rim = jnp.zeros((out_rows, depth), jnp.float32)
    for tap in range(3):
        taken = load_rows(west, pl.ds(7 + tap, out_rows, stride=2)).astype(jnp.bfloat16)
        rim = rim + dot(taken, tap, 0)
    store_rows(shift, pl.ds(7, out_rows, stride=half), rim)
    result = central + load_rows(shift, pl.ds(7, flat))

    @pl.when(lat < n_lat - 1)
    def _():
        for item in downward:
            item.wait_send()

    sideways.wait_send()
    return result


def encode_kernel(
    n_lat, n_lon, height, width, grid_ref, k1_ref, k2_ref, out_ref,
    field1, even1, odd1, col1, west1, corner1, shift1,
    field2, even2, odd2, col2, west2, corner2, shift2, sems,
):
    lat = lax.axis_index("lat")
    lon = lax.axis_index("lon")
    barrier = pltpu.get_barrier_semaphore()
    below = lax.rem(lat + 1, n_lat)
    above = lax.rem(lat + n_lat - 1, n_lat)
    east = lax.rem(lon + 1, n_lon)
    west = lax.rem(lon + n_lon - 1, n_lon)
    peers = [(lat, east), (lat, west), (below, lon), (above, lon), (below, east), (above, west)]
    for peer in peers:
        pl.semaphore_signal(barrier, inc=1, device_id=peer, device_id_type=MESH)
    store_rows(field1, pl.ds(0, height * width), grid_ref[...].astype(jnp.float32))
    pl.semaphore_wait(barrier, len(peers))
    first = conv_stage(0, n_lat, n_lon, lat, lon, field1, k1_ref, height, width,
                       even1, odd1, col1, west1, corner1, shift1, sems)
    hidden = jax.nn.gelu(first).astype(jnp.bfloat16)
    store_rows(field2, pl.ds(0, height * width // 4), hidden.astype(jnp.float32))
    second = conv_stage(4, n_lat, n_lon, lat, lon, field2, k2_ref, height // 2, width // 2,
                        even2, odd2, col2, west2, corner2, shift2, sems)
    out_ref[...] = second.astype(jnp.bfloat16)


def encode(grid, kernel1, kernel2, n_lat, n_lon, height, width):
    depth = grid.shape[1]
    vmem = pl.BlockSpec(memory_space=pltpu.VMEM)

    def scratch(h, w):
        f32 = lambda *shape: pltpu.VMEM(shape, jnp.float32)
        lanes = depth // 128
        return [
            f32(lanes, h * w, 128), f32(h + 1, w // 2, depth), f32(h + 1, w // 2, depth),
            f32(lanes, h, 128), f32(lanes, h + 8, 128), f32(w // 2, depth),
            f32(lanes, h * w // 4 + 8, 128),
        ]

    return pl.pallas_call(
        functools.partial(encode_kernel, n_lat, n_lon, height, width),
        out_shape=jax.ShapeDtypeStruct((height * width // 16, depth), jnp.bfloat16),
        in_specs=[vmem] * 3,
        out_specs=vmem,
        scratch_shapes=scratch(height, width) + scratch(height // 2, width // 2)
        + [pltpu.SemaphoreType.DMA((2, 8))],
        compiler_params=pltpu.CompilerParams(
            collective_id=1, has_side_effects=True, vmem_limit_bytes=48 * MIB
        ),
        name="encode",
    )(grid, kernel1, kernel2)


def body(
    radiances, project_weight, tile_ids, slot_offsets, tile_counts,
    setconv_weights, conv1_weight, conv2_weight,
):
    n_lat = lax.axis_size("lat")
    n_lon = lax.axis_size("lon")
    n = n_lat * n_lon
    obs_count = radiances.shape[0]
    limit = 7 * (obs_count // n) // 2
    cap = -(-limit // 16) * 16
    tile_rows, tile_cols, slot_count = setconv_weights.shape
    channels = project_weight.shape[1]

    place = jnp.arange(obs_count, dtype=jnp.int32) % cap
    pos = (tile_ids * cap + place).reshape(1, obs_count)
    packed = project_pack(radiances.T, project_weight, pos, n * cap)

    lanes = -(-cap // 128) * 128
    turns = -(-obs_count // cap)
    spare = (0, turns * cap - obs_count)
    tiles = jnp.pad(tile_ids, spare, constant_values=-1).reshape(1, turns, cap)
    offsets = jnp.pad(slot_offsets, spare).reshape(1, turns, cap)
    target = jnp.arange(n, dtype=jnp.int32)[:, None, None]
    slots = jnp.max(jnp.where(tiles == target, offsets, -1), axis=1)
    slots = jnp.pad(slots, ((0, 0), (0, lanes - cap)), constant_values=-1)
    slots = slots.reshape(n, 1, lanes)
    live = jnp.arange(slot_count, dtype=jnp.int32) < tile_counts.reshape(-1)[0]
    live = jnp.broadcast_to(live[:, None], (slot_count, 128)).astype(jnp.bfloat16)
    grid = setconv(
        packed.reshape(n, cap, channels), slots, live,
        setconv_weights.reshape(-1, slot_count), n_lat, n_lon,
    )
    out = encode(grid, conv1_weight, conv2_weight, n_lat, n_lon, tile_rows, tile_cols)
    return out.reshape(tile_rows // 4, tile_cols // 4, channels)


def solution(mesh):
    in_specs = (
        P(("lat", "lon"), None),
        P(),
        P(("lat", "lon")),
        P(("lat", "lon")),
        P("lat", "lon"),
        P("lat", "lon", None),
        P(),
        P(),
    )
    out_specs = P("lat", "lon", None)
    return jax.shard_map(body, mesh=mesh, in_specs=in_specs, out_specs=out_specs, check_vma=False)
```

```python
import functools

import jax
import jax.numpy as jnp
from jax import lax
from jax.experimental import pallas as pl
from jax.experimental.pallas import tpu as pltpu
from jax.sharding import PartitionSpec as P

MESH = pl.DeviceIdType.MESH
MIB = 1024 * 1024


def project_pack_kernel(steps, tail, rad_ref, weight_ref, pos_ref, packed_ref, acc_ref, feat_ref):
    step = pl.program_id(0)

    def part(weight, rows):
        return lax.dot_general(
            weight, rows, (((0,), (0,)), ((), ())), preferred_element_type=jnp.float32
        )

    @pl.when(step == 0)
    def _():
        acc_ref[...] = part(weight_ref[...], rad_ref[...])

    @pl.when((step > 0) & (step < steps - 1))
    def _():
        acc_ref[...] += part(weight_ref[...], rad_ref[...])

    @pl.when(step == steps - 1)
    def _():
        last = acc_ref[...] + part(weight_ref[:tail], rad_ref[:tail])
        feat_ref[...] = last.T.astype(jnp.bfloat16)
        total = packed_ref.shape[0]
        chunk = 256 if total % 256 == 0 else 128
        obs = feat_ref.shape[0]

        @pl.loop(0, total // chunk)
        def _(c):
            base = pl.multiple_of(c * chunk, chunk)
            target = lax.broadcasted_iota(jnp.int32, (chunk, obs), 0) + base
            onehot = (target == pos_ref[...]).astype(jnp.float32).astype(jnp.bfloat16)
            packed_ref[pl.ds(base, chunk), :] = jnp.dot(
                onehot, feat_ref[...], preferred_element_type=jnp.float32
            ).astype(jnp.bfloat16)


def project_pack(radiances, weight, pos, total):
    raw, obs = radiances.shape
    channels = weight.shape[1]
    block = 1024
    steps = -(-raw // block)
    return pl.pallas_call(
        functools.partial(project_pack_kernel, steps, raw - (steps - 1) * block),
        grid=(steps,),
        out_shape=jax.ShapeDtypeStruct((total, channels), jnp.bfloat16),
        in_specs=[
            pl.BlockSpec((block, obs), lambda i: (i, 0)),
            pl.BlockSpec((block, channels), lambda i: (i, 0)),
            pl.BlockSpec((1, obs), lambda i: (0, 0)),
        ],
        out_specs=pl.BlockSpec((total, channels), lambda i: (0, 0)),
        scratch_shapes=[
            pltpu.VMEM((channels, obs), jnp.float32),
            pltpu.VMEM((obs, channels), jnp.bfloat16),
        ],
        compiler_params=pltpu.CompilerParams(vmem_limit_bytes=48 * MIB),
        cost_estimate=pl.CostEstimate(
            flops=2 * obs * raw * channels,
            bytes_accessed=2 * (obs * raw + raw * channels + total * channels),
            transcendentals=0,
        ),
        name="project_pack",
    )(radiances, weight, pos)


def density_kernel(w_ref, live_ref, dens_ref):
    dens_ref[...] = jnp.dot(w_ref[...], live_ref[...], preferred_element_type=jnp.float32)


def density(weights, live):
    cells, slot_count = weights.shape
    chunk = 256
    return pl.pallas_call(
        density_kernel,
        grid=(cells // chunk,),
        out_shape=jax.ShapeDtypeStruct((cells, 128), jnp.float32),
        in_specs=[
            pl.BlockSpec((chunk, slot_count), lambda i: (i, 0)),
            pl.BlockSpec((slot_count, 128), lambda i: (0, 0)),
        ],
        out_specs=pl.BlockSpec((chunk, 128), lambda i: (i, 0)),
        compiler_params=pltpu.CompilerParams(vmem_limit_bytes=16 * MIB),
        cost_estimate=pl.CostEstimate(
            flops=2 * cells * slot_count * 128,
            bytes_accessed=2 * cells * slot_count,
            transcendentals=0,
        ),
        name="density",
    )(weights, live)


def setconv_kernel(chunk, rows_ref, slots_ref, dens_ref, w_hbm, out_ref, w_vmem, obs, w_sem):
    cells, slot_count = w_vmem.shape
    chunks = cells // chunk

    def w_copy(c):
        part = pl.ds(pl.multiple_of(c * chunk, chunk), chunk)
        return pltpu.make_async_copy(w_hbm.at[part], w_vmem.at[part], w_sem.at[c])

    @pl.loop(0, chunks)
    def _(c):
        w_copy(c).start()

    width = slots_ref.shape[1]
    part_slots = 128

    @pl.loop(0, slot_count // part_slots)
    def _(c):
        base = pl.multiple_of(c * part_slots, part_slots)
        at = lax.broadcasted_iota(jnp.int32, (part_slots, width), 0) + base
        onehot = (at == slots_ref[...]).astype(jnp.float32).astype(jnp.bfloat16)
        placed = jnp.dot(onehot, rows_ref[...], preferred_element_type=jnp.float32)
        obs[pl.ds(base, part_slots), :] = placed.astype(jnp.bfloat16)

    @pl.loop(0, chunks)
    def _(c):
        w_copy(c).wait()
        part = pl.ds(pl.multiple_of(c * chunk, chunk), chunk)
        numerator = jnp.dot(w_vmem[part, :], obs[...], preferred_element_type=jnp.float32)
        root = jnp.sqrt(dens_ref[part, :])
        root = jnp.concatenate([root] * (numerator.shape[1] // root.shape[1]), axis=1)
        out_ref[part, :] = (numerator / root).astype(jnp.bfloat16)


def setconv(rows, slots, dens, weights):
    channels = rows.shape[1]
    cells, slot_count = weights.shape
    chunk = 256
    vmem = pl.BlockSpec(memory_space=pltpu.VMEM)
    return pl.pallas_call(
        functools.partial(setconv_kernel, chunk),
        out_shape=jax.ShapeDtypeStruct((cells, channels), jnp.bfloat16),
        in_specs=[vmem, vmem, vmem, pl.BlockSpec(memory_space=pl.ANY)],
        out_specs=vmem,
        scratch_shapes=[
            pltpu.VMEM((cells, slot_count), jnp.bfloat16),
            pltpu.VMEM((slot_count, channels), jnp.bfloat16),
            pltpu.SemaphoreType.DMA((cells // chunk,)),
        ],
        compiler_params=pltpu.CompilerParams(vmem_limit_bytes=48 * MIB),
        cost_estimate=pl.CostEstimate(
            flops=4 * cells * slot_count * channels,
            bytes_accessed=2 * cells * slot_count,
            transcendentals=0,
        ),
        name="setconv",
    )(rows, slots, dens, weights)


def load_rows(ref, rows):
    return jnp.concatenate([ref[h, rows, :] for h in range(ref.shape[0])], axis=1)


def store_rows(ref, rows, value):
    for h in range(ref.shape[0]):
        ref[h, rows, :] = value[:, h * 128:(h + 1) * 128]


def conv_stage(first, n_lat, n_lon, lat, lon, field, weight, height, width,
               even, odd, column, west, corner, shift, sems):
    half = width // 2
    depth = even.shape[2]
    pairs = height * half
    even[1:, :, :] = load_rows(field, pl.ds(0, pairs, stride=2)).reshape(height, half, depth)
    odd[1:, :, :] = load_rows(field, pl.ds(1, pairs, stride=2)).reshape(height, half, depth)
    store_rows(column, pl.ds(0, height), load_rows(field, pl.ds(width - 1, height, stride=width)))
    below = lax.rem(lat + 1, n_lat)
    east = lax.rem(lon + 1, n_lon)

    def copy(src, dst, k, device):
        return pltpu.make_async_remote_copy(
            src_ref=src, dst_ref=dst, send_sem=sems.at[0, first + k],
            recv_sem=sems.at[1, first + k], device_id=device, device_id_type=MESH,
        )

    sideways = copy(column, west.at[:, pl.ds(8, height)], 0, (lat, east))
    downward = [
        copy(odd.at[height], odd.at[0], 1, (below, lon)),
        copy(even.at[height], even.at[0], 2, (below, lon)),
        copy(odd.at[height], corner, 3, (below, east)),
    ]

    @pl.when(lat < n_lat - 1)
    def _():
        for item in downward:
            item.start()

    sideways.start()

    @pl.when(lat == 0)
    def _():
        even[0] = jnp.zeros_like(even[0])
        odd[0] = jnp.zeros_like(odd[0])
        corner[...] = jnp.zeros_like(corner)

    out_rows = height // 2
    flat = out_rows * half

    def rows_of(ref, tap):
        start = 1 if tap else 0
        picked = ref[start:start + 2 * out_rows].reshape(out_rows, 2, half, depth)
        return picked[:, tap - start].reshape(flat, depth).astype(jnp.bfloat16)

    def dot(rows, a, b):
        return jnp.dot(rows, weight[a, b], preferred_element_type=jnp.float32)

    central = None
    westward = None
    for tap in (1, 2, 0):
        if tap == 0:
            @pl.when(lat > 0)
            def _():
                for item in downward:
                    item.wait_recv()
        odd_rows = rows_of(odd, tap)
        c = dot(rows_of(even, tap), tap, 1) + dot(odd_rows, tap, 2)
        w = dot(odd_rows, tap, 0)
        central = c if central is None else central + c
        westward = w if westward is None else westward + w
    store_rows(shift, pl.ds(8, flat), westward)
    sideways.wait_recv()
    store_rows(west, pl.ds(7, 1), corner[half - 1:half, :])
    rim = jnp.zeros((out_rows, depth), jnp.float32)
    for tap in range(3):
        taken = load_rows(west, pl.ds(7 + tap, out_rows, stride=2)).astype(jnp.bfloat16)
        rim = rim + dot(taken, tap, 0)
    store_rows(shift, pl.ds(7, out_rows, stride=half), rim)
    result = central + load_rows(shift, pl.ds(7, flat))

    @pl.when(lat < n_lat - 1)
    def _():
        for item in downward:
            item.wait_send()

    sideways.wait_send()
    return result


def encode_kernel(
    n_lat, n_lon, height, width, grid_ref, k1_ref, k2_ref, out_ref,
    field1, even1, odd1, col1, west1, corner1, shift1,
    field2, even2, odd2, col2, west2, corner2, shift2, sems,
):
    lat = lax.axis_index("lat")
    lon = lax.axis_index("lon")
    barrier = pltpu.get_barrier_semaphore()
    below = lax.rem(lat + 1, n_lat)
    above = lax.rem(lat + n_lat - 1, n_lat)
    east = lax.rem(lon + 1, n_lon)
    west = lax.rem(lon + n_lon - 1, n_lon)
    peers = [(lat, east), (lat, west), (below, lon), (above, lon), (below, east), (above, west)]
    for peer in peers:
        pl.semaphore_signal(barrier, inc=1, device_id=peer, device_id_type=MESH)
    store_rows(field1, pl.ds(0, height * width), grid_ref[...].astype(jnp.float32))
    pl.semaphore_wait(barrier, len(peers))
    first = conv_stage(0, n_lat, n_lon, lat, lon, field1, k1_ref, height, width,
                       even1, odd1, col1, west1, corner1, shift1, sems)
    hidden = jax.nn.gelu(first).astype(jnp.bfloat16)
    store_rows(field2, pl.ds(0, height * width // 4), hidden.astype(jnp.float32))
    second = conv_stage(4, n_lat, n_lon, lat, lon, field2, k2_ref, height // 2, width // 2,
                        even2, odd2, col2, west2, corner2, shift2, sems)
    out_ref[...] = second.astype(jnp.bfloat16)


def encode(grid, kernel1, kernel2, n_lat, n_lon, height, width):
    depth = grid.shape[1]
    vmem = pl.BlockSpec(memory_space=pltpu.VMEM)

    def scratch(h, w):
        f32 = lambda *shape: pltpu.VMEM(shape, jnp.float32)
        lanes = depth // 128
        return [
            f32(lanes, h * w, 128), f32(h + 1, w // 2, depth), f32(h + 1, w // 2, depth),
            f32(lanes, h, 128), f32(lanes, h + 8, 128), f32(w // 2, depth),
            f32(lanes, h * w // 4 + 8, 128),
        ]

    return pl.pallas_call(
        functools.partial(encode_kernel, n_lat, n_lon, height, width),
        out_shape=jax.ShapeDtypeStruct((height * width // 16, depth), jnp.bfloat16),
        in_specs=[vmem] * 3,
        out_specs=vmem,
        scratch_shapes=scratch(height, width) + scratch(height // 2, width // 2)
        + [pltpu.SemaphoreType.DMA((2, 8))],
        compiler_params=pltpu.CompilerParams(
            collective_id=0, has_side_effects=True, vmem_limit_bytes=48 * MIB
        ),
        name="encode",
    )(grid, kernel1, kernel2)


def body(
    radiances, project_weight, tile_ids, slot_offsets, tile_counts,
    setconv_weights, conv1_weight, conv2_weight,
):
    n_lat = lax.axis_size("lat")
    n_lon = lax.axis_size("lon")
    n = n_lat * n_lon
    obs_count = radiances.shape[0]
    limit = 7 * (obs_count // n) // 2
    cap = -(-limit // 16) * 16
    tile_rows, tile_cols, slot_count = setconv_weights.shape
    channels = project_weight.shape[1]

    place = jnp.arange(obs_count, dtype=jnp.int32) % cap
    pos = (tile_ids * cap + place).reshape(1, obs_count)
    turns = -(-obs_count // cap)
    spare = (0, turns * cap - obs_count)
    tiles = jnp.pad(tile_ids, spare, constant_values=-1).reshape(1, turns, cap)
    offsets = jnp.pad(slot_offsets, spare).reshape(1, turns, cap)
    target = jnp.arange(n, dtype=jnp.int32)[:, None, None]
    slots = jnp.max(jnp.where(tiles == target, offsets, -1), axis=1)
    slots = lax.all_to_all(slots, ("lat", "lon"), 0, 0, tiled=True).reshape(1, n * cap)

    packed = project_pack(radiances.T, project_weight, pos, n * cap)
    rows = lax.all_to_all(
        packed.reshape(n, cap, channels), ("lat", "lon"), 0, 0, tiled=True
    ).reshape(n * cap, channels)
    live = jnp.arange(slot_count, dtype=jnp.int32) < tile_counts.reshape(-1)[0]
    live = jnp.broadcast_to(live[:, None], (slot_count, 128)).astype(jnp.bfloat16)
    weights = setconv_weights.reshape(-1, slot_count)
    grid = setconv(rows, slots, density(weights, live), weights)
    out = encode(grid, conv1_weight, conv2_weight, n_lat, n_lon, tile_rows, tile_cols)
    return out.reshape(tile_rows // 4, tile_cols // 4, channels)


def solution(mesh):
    in_specs = (
        P(("lat", "lon"), None),
        P(),
        P(("lat", "lon")),
        P(("lat", "lon")),
        P("lat", "lon"),
        P("lat", "lon", None),
        P(),
        P(),
    )
    out_specs = P("lat", "lon", None)
    return jax.shard_map(body, mesh=mesh, in_specs=in_specs, out_specs=out_specs, check_vma=False)
```

```python
import functools

import jax
import jax.numpy as jnp
from jax import lax
from jax.experimental import pallas as pl
from jax.experimental.pallas import tpu as pltpu
from jax.sharding import PartitionSpec as P

MESH = pl.DeviceIdType.MESH
MIB = 1024 * 1024


def project_pack_kernel(steps, tail, rad_ref, weight_ref, pos_ref, packed_ref, acc_ref, feat_ref):
    step = pl.program_id(0)

    def part(weight, rows):
        return lax.dot_general(
            weight, rows, (((0,), (0,)), ((), ())), preferred_element_type=jnp.float32
        )

    @pl.when(step == 0)
    def _():
        acc_ref[...] = part(weight_ref[...], rad_ref[...])

    @pl.when((step > 0) & (step < steps - 1))
    def _():
        acc_ref[...] += part(weight_ref[...], rad_ref[...])

    @pl.when(step == steps - 1)
    def _():
        last = acc_ref[...] + part(weight_ref[:tail], rad_ref[:tail])
        feat_ref[...] = last.T.astype(jnp.bfloat16)
        total = packed_ref.shape[0]
        chunk = 512 if total % 512 == 0 else 128
        obs = feat_ref.shape[0]

        @pl.loop(0, total // chunk)
        def _(c):
            base = pl.multiple_of(c * chunk, chunk)
            target = lax.broadcasted_iota(jnp.int32, (chunk, obs), 0) + base
            onehot = (target == pos_ref[...]).astype(jnp.float32).astype(jnp.bfloat16)
            packed_ref[pl.ds(base, chunk), :] = jnp.dot(
                onehot, feat_ref[...], preferred_element_type=jnp.float32
            ).astype(jnp.bfloat16)


def project_pack(radiances, weight, pos, total):
    raw, obs = radiances.shape
    channels = weight.shape[1]
    block = 2048
    steps = -(-raw // block)
    return pl.pallas_call(
        functools.partial(project_pack_kernel, steps, raw - (steps - 1) * block),
        grid=(steps,),
        out_shape=jax.ShapeDtypeStruct((total, channels), jnp.bfloat16),
        in_specs=[
            pl.BlockSpec((block, obs), lambda i: (i, 0)),
            pl.BlockSpec((block, channels), lambda i: (i, 0)),
            pl.BlockSpec((1, obs), lambda i: (0, 0)),
        ],
        out_specs=pl.BlockSpec((total, channels), lambda i: (0, 0)),
        scratch_shapes=[
            pltpu.VMEM((channels, obs), jnp.float32),
            pltpu.VMEM((obs, channels), jnp.bfloat16),
        ],
        compiler_params=pltpu.CompilerParams(vmem_limit_bytes=60 * MIB),
        cost_estimate=pl.CostEstimate(
            flops=2 * obs * raw * channels,
            bytes_accessed=2 * (obs * raw + raw * channels + total * channels),
            transcendentals=0,
        ),
        name="project_pack",
    )(radiances, weight, pos)


def density_kernel(w_ref, live_ref, dens_ref):
    dens_ref[...] = jnp.dot(w_ref[...], live_ref[...], preferred_element_type=jnp.float32)


def density(weights, live):
    cells, slot_count = weights.shape
    chunk = 256
    return pl.pallas_call(
        density_kernel,
        grid=(cells // chunk,),
        out_shape=jax.ShapeDtypeStruct((cells, 128), jnp.float32),
        in_specs=[
            pl.BlockSpec((chunk, slot_count), lambda i: (i, 0)),
            pl.BlockSpec((slot_count, 128), lambda i: (0, 0)),
        ],
        out_specs=pl.BlockSpec((chunk, 128), lambda i: (i, 0)),
        compiler_params=pltpu.CompilerParams(vmem_limit_bytes=16 * MIB),
        cost_estimate=pl.CostEstimate(
            flops=2 * cells * slot_count * 128,
            bytes_accessed=2 * cells * slot_count,
            transcendentals=0,
        ),
        name="density",
    )(weights, live)


def setconv_kernel(chunk, rows_ref, slots_ref, dens_ref, w_hbm, out_ref, w_vmem, obs, w_sem):
    cells, slot_count = w_vmem.shape
    chunks = cells // chunk

    def w_copy(c):
        part = pl.ds(pl.multiple_of(c * chunk, chunk), chunk)
        return pltpu.make_async_copy(w_hbm.at[part], w_vmem.at[part], w_sem.at[c])

    @pl.loop(0, chunks)
    def _(c):
        w_copy(c).start()

    width = slots_ref.shape[1]
    part_slots = 512

    @pl.loop(0, slot_count // part_slots)
    def _(c):
        base = pl.multiple_of(c * part_slots, part_slots)
        at = lax.broadcasted_iota(jnp.int32, (part_slots, width), 0) + base
        onehot = (at == slots_ref[...]).astype(jnp.float32).astype(jnp.bfloat16)
        placed = jnp.dot(onehot, rows_ref[...], preferred_element_type=jnp.float32)
        obs[pl.ds(base, part_slots), :] = placed.astype(jnp.bfloat16)

    @pl.loop(0, chunks)
    def _(c):
        w_copy(c).wait()
        part = pl.ds(pl.multiple_of(c * chunk, chunk), chunk)
        numerator = jnp.dot(w_vmem[part, :], obs[...], preferred_element_type=jnp.float32)
        root = jnp.sqrt(dens_ref[part, :])
        root = jnp.concatenate([root] * (numerator.shape[1] // root.shape[1]), axis=1)
        out_ref[part, :] = (numerator / root).astype(jnp.bfloat16)


def setconv(rows, slots, dens, weights):
    channels = rows.shape[1]
    cells, slot_count = weights.shape
    chunk = 512
    vmem = pl.BlockSpec(memory_space=pltpu.VMEM)
    return pl.pallas_call(
        functools.partial(setconv_kernel, chunk),
        out_shape=jax.ShapeDtypeStruct((cells, channels), jnp.bfloat16),
        in_specs=[vmem, vmem, vmem, pl.BlockSpec(memory_space=pl.ANY)],
        out_specs=vmem,
        scratch_shapes=[
            pltpu.VMEM((cells, slot_count), jnp.bfloat16),
            pltpu.VMEM((slot_count, channels), jnp.bfloat16),
            pltpu.SemaphoreType.DMA((cells // chunk,)),
        ],
        compiler_params=pltpu.CompilerParams(vmem_limit_bytes=48 * MIB),
        cost_estimate=pl.CostEstimate(
            flops=4 * cells * slot_count * channels,
            bytes_accessed=2 * cells * slot_count,
            transcendentals=0,
        ),
        name="setconv",
    )(rows, slots, dens, weights)


def load_rows(ref, rows):
    return jnp.concatenate([ref[h, rows, :] for h in range(ref.shape[0])], axis=1)


def store_rows(ref, rows, value):
    for h in range(ref.shape[0]):
        ref[h, rows, :] = value[:, h * 128:(h + 1) * 128]


def conv_stage(first, n_lat, n_lon, lat, lon, field, weight, height, width,
               even, odd, column, west, corner, shift, sems):
    half = width // 2
    depth = even.shape[2]
    pairs = height * half
    even[1:, :, :] = load_rows(field, pl.ds(0, pairs, stride=2)).reshape(height, half, depth)
    odd[1:, :, :] = load_rows(field, pl.ds(1, pairs, stride=2)).reshape(height, half, depth)
    store_rows(column, pl.ds(0, height), load_rows(field, pl.ds(width - 1, height, stride=width)))
    below = lax.rem(lat + 1, n_lat)
    east = lax.rem(lon + 1, n_lon)

    def copy(src, dst, k, device):
        return pltpu.make_async_remote_copy(
            src_ref=src, dst_ref=dst, send_sem=sems.at[0, first + k],
            recv_sem=sems.at[1, first + k], device_id=device, device_id_type=MESH,
        )

    sideways = copy(column, west.at[:, pl.ds(8, height)], 0, (lat, east))
    downward = [
        copy(odd.at[height], odd.at[0], 1, (below, lon)),
        copy(even.at[height], even.at[0], 2, (below, lon)),
        copy(odd.at[height], corner, 3, (below, east)),
    ]

    @pl.when(lat < n_lat - 1)
    def _():
        for item in downward:
            item.start()

    sideways.start()

    @pl.when(lat == 0)
    def _():
        even[0] = jnp.zeros_like(even[0])
        odd[0] = jnp.zeros_like(odd[0])
        corner[...] = jnp.zeros_like(corner)

    out_rows = height // 2
    flat = out_rows * half

    def rows_of(ref, tap):
        start = 1 if tap else 0
        picked = ref[start:start + 2 * out_rows].reshape(out_rows, 2, half, depth)
        return picked[:, tap - start].reshape(flat, depth).astype(jnp.bfloat16)

    def dot(rows, a, b):
        return jnp.dot(rows, weight[a, b], preferred_element_type=jnp.float32)

    central = None
    westward = None
    for tap in (1, 2, 0):
        if tap == 0:
            @pl.when(lat > 0)
            def _():
                for item in downward:
                    item.wait_recv()
        odd_rows = rows_of(odd, tap)
        c = dot(rows_of(even, tap), tap, 1) + dot(odd_rows, tap, 2)
        w = dot(odd_rows, tap, 0)
        central = c if central is None else central + c
        westward = w if westward is None else westward + w
    store_rows(shift, pl.ds(8, flat), westward)
    sideways.wait_recv()
    store_rows(west, pl.ds(7, 1), corner[half - 1:half, :])
    rim = jnp.zeros((out_rows, depth), jnp.float32)
    for tap in range(3):
        taken = load_rows(west, pl.ds(7 + tap, out_rows, stride=2)).astype(jnp.bfloat16)
        rim = rim + dot(taken, tap, 0)
    store_rows(shift, pl.ds(7, out_rows, stride=half), rim)
    result = central + load_rows(shift, pl.ds(7, flat))

    @pl.when(lat < n_lat - 1)
    def _():
        for item in downward:
            item.wait_send()

    sideways.wait_send()
    return result


def encode_kernel(
    n_lat, n_lon, height, width, grid_ref, k1_ref, k2_ref, out_ref,
    field1, even1, odd1, col1, west1, corner1, shift1,
    field2, even2, odd2, col2, west2, corner2, shift2, sems,
):
    lat = lax.axis_index("lat")
    lon = lax.axis_index("lon")
    barrier = pltpu.get_barrier_semaphore()
    below = lax.rem(lat + 1, n_lat)
    above = lax.rem(lat + n_lat - 1, n_lat)
    east = lax.rem(lon + 1, n_lon)
    west = lax.rem(lon + n_lon - 1, n_lon)
    peers = [(lat, east), (lat, west), (below, lon), (above, lon), (below, east), (above, west)]
    for peer in peers:
        pl.semaphore_signal(barrier, inc=1, device_id=peer, device_id_type=MESH)
    store_rows(field1, pl.ds(0, height * width), grid_ref[...].astype(jnp.float32))
    pl.semaphore_wait(barrier, len(peers))
    first = conv_stage(0, n_lat, n_lon, lat, lon, field1, k1_ref, height, width,
                       even1, odd1, col1, west1, corner1, shift1, sems)
    hidden = jax.nn.gelu(first).astype(jnp.bfloat16)
    store_rows(field2, pl.ds(0, height * width // 4), hidden.astype(jnp.float32))
    second = conv_stage(4, n_lat, n_lon, lat, lon, field2, k2_ref, height // 2, width // 2,
                        even2, odd2, col2, west2, corner2, shift2, sems)
    out_ref[...] = second.astype(jnp.bfloat16)


def encode(grid, kernel1, kernel2, n_lat, n_lon, height, width):
    depth = grid.shape[1]
    vmem = pl.BlockSpec(memory_space=pltpu.VMEM)

    def scratch(h, w):
        f32 = lambda *shape: pltpu.VMEM(shape, jnp.float32)
        lanes = depth // 128
        return [
            f32(lanes, h * w, 128), f32(h + 1, w // 2, depth), f32(h + 1, w // 2, depth),
            f32(lanes, h, 128), f32(lanes, h + 8, 128), f32(w // 2, depth),
            f32(lanes, h * w // 4 + 8, 128),
        ]

    return pl.pallas_call(
        functools.partial(encode_kernel, n_lat, n_lon, height, width),
        out_shape=jax.ShapeDtypeStruct((height * width // 16, depth), jnp.bfloat16),
        in_specs=[vmem] * 3,
        out_specs=vmem,
        scratch_shapes=scratch(height, width) + scratch(height // 2, width // 2)
        + [pltpu.SemaphoreType.DMA((2, 8))],
        compiler_params=pltpu.CompilerParams(
            collective_id=0, has_side_effects=True, vmem_limit_bytes=48 * MIB
        ),
        name="encode",
    )(grid, kernel1, kernel2)


def body(
    radiances, project_weight, tile_ids, slot_offsets, tile_counts,
    setconv_weights, conv1_weight, conv2_weight,
):
    n_lat = lax.axis_size("lat")
    n_lon = lax.axis_size("lon")
    n = n_lat * n_lon
    obs_count = radiances.shape[0]
    limit = 7 * (obs_count // n) // 2
    cap = -(-limit // 16) * 16
    tile_rows, tile_cols, slot_count = setconv_weights.shape
    channels = project_weight.shape[1]

    place = jnp.arange(obs_count, dtype=jnp.int32) % cap
    pos = (tile_ids * cap + place).reshape(1, obs_count)
    turns = -(-obs_count // cap)
    spare = (0, turns * cap - obs_count)
    tiles = jnp.pad(tile_ids, spare, constant_values=-1).reshape(1, turns, cap)
    offsets = jnp.pad(slot_offsets, spare).reshape(1, turns, cap)
    target = jnp.arange(n, dtype=jnp.int32)[:, None, None]
    slots = jnp.max(jnp.where(tiles == target, offsets, -1), axis=1)
    slots = lax.all_to_all(slots, ("lat", "lon"), 0, 0, tiled=True).reshape(1, n * cap)

    packed = project_pack(radiances.T, project_weight, pos, n * cap)
    rows = lax.all_to_all(
        packed.reshape(n, cap, channels), ("lat", "lon"), 0, 0, tiled=True
    ).reshape(n * cap, channels)
    live = jnp.arange(slot_count, dtype=jnp.int32) < tile_counts.reshape(-1)[0]
    live = jnp.broadcast_to(live[:, None], (slot_count, 128)).astype(jnp.bfloat16)
    weights = setconv_weights.reshape(-1, slot_count)
    grid = setconv(rows, slots, density(weights, live), weights)
    out = encode(grid, conv1_weight, conv2_weight, n_lat, n_lon, tile_rows, tile_cols)
    return out.reshape(tile_rows // 4, tile_cols // 4, channels)


def solution(mesh):
    in_specs = (
        P(("lat", "lon"), None),
        P(),
        P(("lat", "lon")),
        P(("lat", "lon")),
        P("lat", "lon"),
        P("lat", "lon", None),
        P(),
        P(),
    )
    out_specs = P("lat", "lon", None)
    return jax.shard_map(body, mesh=mesh, in_specs=in_specs, out_specs=out_specs, check_vma=False)
```
